128 devices in a mesh: row: 32 (over z, x, core), grp: 4 (over y).
Axes of the slice: x: 4, y: 4, z: 4, core: 2. Of those that a mesh axis runs over, the one named last changes fastest.
Arguments:
- inputs: bfloat16 [1048576, 512], P(('row', 'grp')), may hold values from -6 to 6
- frequencies: bfloat16 [512, 512], replicated, may hold values from -0.25 to 0.25
- phases: float32 [512], replicated, may hold values from -3.140625 to 3.140625
- targets: bfloat16 [1048576, 128], P(('row', 'grp')), may hold values from -9 to 9
Outputs:
- weights: float32 [512, 128], P('grp', 'row')
The draws below stay inside these ranges and needn't reach their ends.
All inputs are finite; a program needn't handle non-finite values.
Results may differ from the reference program's by a relative error of at most 0.0036.
Values sent between devices are 32-bit elements; how exact they have to be, the bound alone decides.
No kernel may reach another device: no remote copies, remote signals or barrier semaphores. Data moves between devices by JAX's collectives and lax.ppermute only.
A program may use at most 192 MiB of HBM per device.

```python
import jax
import jax.numpy as jnp
from jax import lax

IN = 512
FEATURES = 512
OUTS = 128
ROWS_DEV = 8192
COLS = 640
ROWS = 1048576
N_ROW = 32
N_GRP = 4


def draw_targets(key, part):
    key = jax.random.fold_in(key, 7)
    position = jnp.arange(ROWS, dtype=jnp.float32)[:, None]
    scale = 1.0 + 2.0 * position / (ROWS - 1)
    noise = jnp.clip(jax.random.normal(key, (ROWS, OUTS), jnp.float32), -3.0, 3.0)
    return (noise * scale).astype(jnp.bfloat16)


def levels(key, shape, cuts, low, largest):
    def one(dim, blocks):
        draws = jax.random.uniform(jax.random.fold_in(jax.random.fold_in(key, 6), dim), (blocks,), jnp.float32, low / len(cuts), largest / len(cuts))
        return jnp.repeat(jnp.exp(draws), shape[dim] // blocks).reshape((-1,) + (1,) * (len(shape) - dim - 1))

    factor_of = one(*cuts[0])
    for cut in cuts[1:]:
        factor_of = factor_of * one(*cut)
    return factor_of


def normal_values(own_key, extent, deviation, reach, cuts=(), kind=jnp.bfloat16):
    drawn = jax.random.normal(own_key, extent, jnp.float32) * deviation
    if len(cuts) > 0:
        drawn = levels(own_key, extent, cuts, -0.22, 0.18) * drawn
    return jnp.clip(drawn, min=-reach, max=reach).astype(kind)


def setup_inputs(seed: int = 0) -> dict:
    key_list = jax.random.split(jax.random.key(seed), 5)
    inputs = normal_values(key_list[0], (ROWS, IN), 1.0, 6.0, ((0, 128),))
    frequencies = normal_values(key_list[1], (IN, FEATURES), IN ** -0.5, 0.25)
    phases = jnp.clip(jax.random.uniform(key_list[2], (FEATURES,), jnp.float32, -3.140625, 3.140625), -3.140625, 3.140625)
    targets = draw_targets(jax.random.fold_in(key_list[4], 71), 0)
    return dict(inputs=inputs, frequencies=frequencies, phases=phases, targets=targets)


def reference(inputs, frequencies, phases, targets):
    blocks = N_ROW * N_GRP
    xs = inputs.reshape(blocks, ROWS_DEV, IN)
    ys = targets.reshape(blocks, ROWS_DEV, OUTS)

    def step(carry, pair):
        block_x, block_y = pair
        projected = jnp.dot(block_x.astype(jnp.float32), frequencies.astype(jnp.float32), preferred_element_type=jnp.float32)
        features = (jnp.sqrt(2.0 / FEATURES) * jnp.cos(projected + phases)).astype(jnp.bfloat16)
        table = jnp.concatenate([features, block_y], axis=1)
        return (carry + jnp.dot(table.T.astype(jnp.float32), table.astype(jnp.float32), preferred_element_type=jnp.float32), None)
    gram, unused = lax.scan(step, jnp.zeros((COLS, COLS), jnp.float32), (xs, ys))
    ridge = 0.25 * ROWS / FEATURES
    system = gram[:FEATURES, :FEATURES] + ridge * jnp.eye(FEATURES, dtype=jnp.float32)
    right = gram[:FEATURES, FEATURES:]
    lower = jnp.linalg.cholesky(system)
    middle = lax.linalg.triangular_solve(lower, right, left_side=True, lower=True)
    solved = lax.linalg.triangular_solve(lower, middle, left_side=True, lower=True, transpose_a=True)
    return solved * jnp.sqrt(ROWS / FEATURES)
```

```python
import jax
import jax.numpy as jnp
import numpy as np
from jax import lax
from jax.sharding import Mesh, PartitionSpec as P

CHIPS = ("z", "x", "y")


def blocked_cholesky(matrix):
    order_count = matrix.shape[0]
    panel_width = min(128, order_count)
    trailing = matrix
    panels = []
    for offset in range(0, order_count, panel_width):
        pivot_block = jnp.linalg.cholesky(trailing[:panel_width, :panel_width])
        pieces = [jnp.zeros((offset, panel_width), jnp.float32), pivot_block]
        if offset + panel_width < order_count:
            below_block = lax.linalg.triangular_solve(
                pivot_block,
                trailing[panel_width:, :panel_width],
                left_side=False,
                lower=True,
                transpose_a=True,
            )
            pieces.append(below_block)
            update = lax.dot_general(
                below_block,
                below_block,
                (((1,), (1,)), ((), ())),
                precision=lax.Precision.HIGHEST,
                preferred_element_type=jnp.float32,
            )
            trailing = trailing[panel_width:, panel_width:] - update
        panels.append(jnp.concatenate(pieces, axis=0))
    return jnp.concatenate(panels, axis=1)


def sine_coefficients(scale):
    nodes = np.cos((np.arange(64) + 0.5) * np.pi / 64) * 0.25
    powers = np.stack([nodes ** (2 * k + 1) for k in range(5)], axis=1)
    fitted = np.linalg.lstsq(powers / nodes[:, None], np.sin(2 * np.pi * nodes) / nodes, rcond=None)[0]
    return [float(scale * c) for c in fitted]


def scaled_cosine(angle, scale):
    turns = angle * np.float32(1 / (2 * np.pi))
    turns = turns - jnp.round(turns)
    quarter = 0.25 - jnp.abs(turns)
    square = quarter * quarter
    c = sine_coefficients(scale)
    series = c[3] + square * c[4]
    series = c[2] + square * series
    series = c[1] + square * series
    series = c[0] + square * series
    return quarter * series


def sum_over_devices(parts):
    core = lax.axis_index("core")
    swap = [(0, 1), (1, 0)]
    other = lax.ppermute(lax.dynamic_index_in_dim(parts, 1 - core, keepdims=False), "core", swap)
    half = lax.dynamic_index_in_dim(parts, core, keepdims=False) + other
    chunks = lax.all_to_all(half.reshape(64, 16, 128), CHIPS, 0, 0, tiled=True)
    total = jnp.sum(chunks, axis=0, keepdims=True)
    gathered = lax.all_to_all(jnp.broadcast_to(total, (64, 16, 128)), CHIPS, 0, 0, tiled=True)
    mine = gathered.reshape(1024, 128)
    theirs = lax.ppermute(mine, "core", swap)
    first = jnp.where(core == 0, mine, theirs)
    second = jnp.where(core == 0, theirs, mine)
    return first, second


def body(inputs, frequencies, phases, targets):
    feature_count = frequencies.shape[1]
    projected = jnp.dot(inputs, frequencies, preferred_element_type=jnp.float32)
    features = scaled_cosine(projected + phases, np.sqrt(2.0 / feature_count)).astype(jnp.bfloat16)

    def cross(a, b):
        return lax.dot_general(a, b, (((0,), (0,)), ((), ())), preferred_element_type=jnp.float32)

    left = features[:, :256]
    late = features[:, 256:]
    a = cross(left, left)
    b = cross(late, features)
    r = cross(features, targets)
    parts = jnp.stack(
        [
            jnp.concatenate([a[:, :128], a[:, 128:], r], axis=0),
            jnp.concatenate([b[:, :128], b[:, 128:256], b[:, 256:384], b[:, 384:]], axis=0),
        ]
    )
    first, second = sum_over_devices(parts)
    a = jnp.concatenate([first[:256], first[256:512]], axis=1)
    right = first[512:]
    b = jnp.concatenate([second[:256], second[256:512]], axis=1)
    d = jnp.concatenate([second[512:768], second[768:]], axis=1)
    gram = jnp.concatenate(
        [jnp.concatenate([a, b.T], axis=1), jnp.concatenate([b, d], axis=1)], axis=0
    )
    total_rows = inputs.shape[0] * 128
    ridge = 0.25 * total_rows / feature_count
    system = gram + ridge * jnp.eye(feature_count, dtype=jnp.float32)
    lower = blocked_cholesky(system)
    middle = lax.linalg.triangular_solve(lower, right, left_side=True, lower=True)
    solved = lax.linalg.triangular_solve(
        lower, middle, left_side=True, lower=True, transpose_a=True
    )
    solved = solved * jnp.sqrt(total_rows / feature_count)
    feature_start = lax.axis_index("y") * 128
    target_start = lax.axis_index(("z", "x", "core")) * 4
    return lax.dynamic_slice(solved, (feature_start, target_start), (128, 4))


def solution(mesh):
    split = Mesh(mesh.devices.reshape(4, 4, 2, 4), ("z", "x", "core", "y"))
    rows = ("z", "x", "core", "y")
    return jax.shard_map(
        body,
        mesh=split,
        in_specs=(P(rows, None), P(), P(), P(rows, None)),
        out_specs=P("y", ("z", "x", "core")),
        check_vma=False,
    )
```

```python
import functools

import jax
import jax.numpy as jnp
import numpy as np
from jax import lax
from jax.experimental import pallas as pl
from jax.experimental.pallas import tpu as pltpu
from jax.sharding import Mesh, PartitionSpec as P

CHIPS = ("z", "x", "y")
HIGHEST = lax.Precision.HIGHEST


def dot32(a, b, dims=((1,), (0,))):
    return lax.dot_general(a, b, (dims, ((), ())), precision=HIGHEST, preferred_element_type=jnp.float32)

def halves(v):
    high = v.astype(jnp.bfloat16)
    return high, (v - high.astype(jnp.float32)).astype(jnp.bfloat16)

def dot16(a, b):
    return jnp.dot(a, b, preferred_element_type=jnp.float32)

def dot_split(a, b):
    (ah, al), (bh, bl) = a, b
    return dot16(ah, bh) + (dot16(ah, bl) + dot16(al, bh))

def spectrum_steps(low, high, small):
    middle = 2.0 / (low + high)
    reach = (high - low) / (high + low)
    scales = []
    while reach > small:
        scales.append(2.0 / (2.0 - reach * reach))
        reach = reach * reach / (2.0 - reach * reach)
    return middle, scales

def inverse_of(a, eye, low, high, small=1e-3, polish=2):
    middle, scales = spectrum_steps(low, high, small)
    y = middle * a
    yy = halves(y)
    x = (2.0 * middle * scales[0]) * eye - (middle * scales[0]) * y
    y = scales[0] * (2.0 * y - dot_split(yy, yy))
    for s in scales[1:-1]:
        yy = halves(y); xx = halves(x)
        x = s * (2.0 * x - dot_split(xx, yy))
        y = s * (2.0 * y - dot_split(yy, yy))
    s = scales[-1]
    x = s * (2.0 * x - dot_split(halves(x), halves(y)))
    for _ in range(polish):
        miss = eye - dot32(a, x)
        x = x + dot_split(halves(x), halves(miss))
    return x

def solve_kernel(low, high, ridge, scale, spots_ref, mine_ref, theirs_ref, out_ref, g_ref):
    @pl.when(spots_ref[0] == 0)
    def _():
        g_ref[0] = mine_ref[...]
        g_ref[1] = theirs_ref[...]
    @pl.when(spots_ref[0] != 0)
    def _():
        g_ref[0] = theirs_ref[...]
        g_ref[1] = mine_ref[...]
    rows = lax.broadcasted_iota(jnp.int32, (256, 256), 0)
    cols = lax.broadcasted_iota(jnp.int32, (256, 256), 1)
    eye = jnp.where(rows == cols, 1.0, 0.0).astype(jnp.float32)
    a = jnp.concatenate([g_ref[0, :256], g_ref[0, 256:512]], axis=1) + ridge * eye
    b = jnp.concatenate([g_ref[1, :256], g_ref[1, 256:512]], axis=1)
    c = jnp.concatenate([g_ref[1, 512:768], g_ref[1, 768:]], axis=1) + ridge * eye
    pick = pl.multiple_of(spots_ref[1], 8)
    r1 = jnp.concatenate([g_ref[0, pl.ds(512 + pick, 8)], g_ref[0, pl.ds(640 + pick, 8)]], axis=1)
    r2 = jnp.concatenate([g_ref[0, pl.ds(768 + pick, 8)], g_ref[0, pl.ds(896 + pick, 8)]], axis=1)
    xa = inverse_of(a, eye, low, high)
    t = dot32(b, xa)
    s = c - dot32(t, b, ((1,), (1,)))
    r2 = r2 - dot32(r1, t, ((1,), (1,)))
    xs = inverse_of(s, eye, low, high)
    w2 = dot32(r2, xs)
    w1 = dot32(r1 - dot32(w2, b), xa)
    w = scale * jnp.concatenate([w1, w2], axis=1)
    w = jnp.where(spots_ref[2] == 0, w[:4], w[4:])
    block = spots_ref[3]
    out = w[:, :128]
    for k in range(1, 4):
        out = jnp.where(block == k, w[:, 128 * k:128 * (k + 1)], out)
    out_ref[...] = out

def solve(spots, mine, theirs, ridge, scale):
    low = 0.98 * ridge
    high = 1.01 * (256 * 8 + 1) * ridge
    return pl.pallas_call(
        functools.partial(solve_kernel, low, high, ridge, scale),
        out_shape=jax.ShapeDtypeStruct((4, 128), jnp.float32),
        in_specs=[
            pl.BlockSpec(memory_space=pltpu.SMEM),
            pl.BlockSpec(memory_space=pltpu.VMEM),
            pl.BlockSpec(memory_space=pltpu.VMEM),
        ],
        scratch_shapes=[pltpu.VMEM((2, 1024, 128), jnp.float32)],
        name="solve",
        compiler_params=pltpu.CompilerParams(vmem_limit_bytes=40 * 2**20),
    )(spots, mine, theirs)


def sine_coefficients(scale):
    nodes = np.cos((np.arange(64) + 0.5) * np.pi / 64) * 0.25
    powers = np.stack([nodes ** (2 * k + 1) for k in range(5)], axis=1)
    fitted = np.linalg.lstsq(powers / nodes[:, None], np.sin(2 * np.pi * nodes) / nodes, rcond=None)[0]
    return [float(scale * c) for c in fitted]


def scaled_cosine(angle, scale):
    turns = angle * np.float32(1 / (2 * np.pi))
    turns = turns - jnp.round(turns)
    quarter = 0.25 - jnp.abs(turns)
    square = quarter * quarter
    c = sine_coefficients(scale)
    series = c[3] + square * c[4]
    series = c[2] + square * series
    series = c[1] + square * series
    series = c[0] + square * series
    return quarter * series


def sum_over_devices(parts):
    core = lax.axis_index("core")
    swap = [(0, 1), (1, 0)]
    other = lax.ppermute(lax.dynamic_index_in_dim(parts, 1 - core, keepdims=False), "core", swap)
    half = lax.dynamic_index_in_dim(parts, core, keepdims=False) + other
    chunks = lax.all_to_all(half.reshape(64, 16, 128), CHIPS, 0, 0, tiled=True)
    total = jnp.sum(chunks, axis=0, keepdims=True)
    gathered = lax.all_to_all(jnp.broadcast_to(total, (64, 16, 128)), CHIPS, 0, 0, tiled=True)
    mine = gathered.reshape(1024, 128)
    return mine, lax.ppermute(mine, "core", swap)


def body(inputs, frequencies, phases, targets):
    feature_count = frequencies.shape[1]
    projected = jnp.dot(inputs, frequencies, preferred_element_type=jnp.float32)
    features = scaled_cosine(projected + phases, np.sqrt(2.0 / feature_count)).astype(jnp.bfloat16)

    def cross(a, b):
        return lax.dot_general(a, b, (((0,), (0,)), ((), ())), preferred_element_type=jnp.float32)

    left = features[:, :256]
    late = features[:, 256:]
    a = cross(left, left)
    b = cross(late, features)
    r = cross(targets, features)
    parts = jnp.stack(
        [
            jnp.concatenate([a[:, :128], a[:, 128:], r[:, :128], r[:, 128:256], r[:, 256:384], r[:, 384:]]),
            jnp.concatenate([b[:, :128], b[:, 128:256], b[:, 256:384], b[:, 384:]]),
        ]
    )
    mine, theirs = sum_over_devices(parts)
    total_rows = inputs.shape[0] * 128
    ridge = 0.25 * total_rows / feature_count
    group = lax.axis_index(("z", "x", "core"))
    spots = jnp.stack([lax.axis_index("core"), group // 2 * 8, group % 2, lax.axis_index("y")])
    return solve(spots.astype(jnp.int32), mine, theirs, ridge, np.sqrt(total_rows / feature_count)).T


def solution(mesh):
    split = Mesh(mesh.devices.reshape(4, 4, 2, 4), ("z", "x", "core", "y"))
    rows = ("z", "x", "core", "y")
    return jax.shard_map(
        body,
        mesh=split,
        in_specs=(P(rows, None), P(), P(), P(rows, None)),
        out_specs=P("y", ("z", "x", "core")),
        check_vma=False,
    )
```

```python
import functools

import jax
import jax.numpy as jnp
import numpy as np
from jax import lax
from jax.experimental import pallas as pl
from jax.experimental.pallas import tpu as pltpu
from jax.sharding import Mesh, PartitionSpec as P

CHIPS = ("z", "x", "y")
HIGHEST = lax.Precision.HIGHEST


def dot32(a, b, dims=((1,), (0,))):
    return lax.dot_general(a, b, (dims, ((), ())), precision=HIGHEST, preferred_element_type=jnp.float32)

def halves(v):
    high = v.astype(jnp.bfloat16)
    return high, (v - high.astype(jnp.float32)).astype(jnp.bfloat16)

def dot16(a, b):
    return jnp.dot(a, b, preferred_element_type=jnp.float32)

def dot_split(a, b):
    (ah, al), (bh, bl) = a, b
    return dot16(ah, bh) + (dot16(ah, bl) + dot16(al, bh))

def spectrum_steps(low, high, small):
    middle = 2.0 / (low + high)
    reach = (high - low) / (high + low)
    scales = []
    while reach > small:
        scales.append(2.0 / (2.0 - reach * reach))
        reach = reach * reach / (2.0 - reach * reach)
    return middle, scales

def inverse_of(a, eye, low, high, small=1e-3, polish=2):
    middle, scales = spectrum_steps(low, high, small)
    y = middle * a
    yy = halves(y)
    x = (2.0 * middle * scales[0]) * eye - (middle * scales[0]) * y
    y = scales[0] * (2.0 * y - dot_split(yy, yy))
    for s in scales[1:-1]:
        yy = halves(y); xx = halves(x)
        x = s * (2.0 * x - dot_split(xx, yy))
        y = s * (2.0 * y - dot_split(yy, yy))
    s = scales[-1]
    x = s * (2.0 * x - dot_split(halves(x), halves(y)))
    for _ in range(polish):
        miss = eye - dot32(a, x)
        x = x + dot_split(halves(x), halves(miss))
    return x

def solve_kernel(low, high, ridge, scale, spots_ref, mine_ref, theirs_ref, out_ref, g_ref):
    @pl.when(spots_ref[0] == 0)
    def _():
        g_ref[0] = mine_ref[...]
        g_ref[1] = theirs_ref[...]
    @pl.when(spots_ref[0] != 0)
    def _():
        g_ref[0] = theirs_ref[...]
        g_ref[1] = mine_ref[...]
    rows = lax.broadcasted_iota(jnp.int32, (256, 256), 0)
    cols = lax.broadcasted_iota(jnp.int32, (256, 256), 1)
    eye = jnp.where(rows == cols, 1.0, 0.0).astype(jnp.float32)
    a = jnp.concatenate([g_ref[0, :256], g_ref[0, 256:512]], axis=1) + ridge * eye
    b = jnp.concatenate([g_ref[1, :256], g_ref[1, 256:512]], axis=1)
    c = jnp.concatenate([g_ref[1, 512:768], g_ref[1, 768:]], axis=1) + ridge * eye
    pick = pl.multiple_of(spots_ref[1], 8)
    r1 = jnp.concatenate([g_ref[0, pl.ds(512 + pick, 8)], g_ref[0, pl.ds(640 + pick, 8)]], axis=1)
    r2 = jnp.concatenate([g_ref[0, pl.ds(768 + pick, 8)], g_ref[0, pl.ds(896 + pick, 8)]], axis=1)
    xa = inverse_of(a, eye, low, high)
    t = dot32(b, xa)
    s = c - dot32(t, b, ((1,), (1,)))
    r2 = r2 - dot32(r1, t, ((1,), (1,)))
    xs = inverse_of(s, eye, low, high)
    w2 = dot32(r2, xs)
    w1 = dot32(r1 - dot32(w2, b), xa)
    w = scale * jnp.concatenate([w1, w2], axis=1)
    w = jnp.where(spots_ref[2] == 0, w[:4], w[4:])
    block = spots_ref[3]
    out = w[:, :128]
    for k in range(1, 4):
        out = jnp.where(block == k, w[:, 128 * k:128 * (k + 1)], out)
    out_ref[...] = out

def solve(spots, mine, theirs, ridge, scale):
    low = 0.98 * ridge
    high = 1.01 * (256 * 8 + 1) * ridge
    return pl.pallas_call(
        functools.partial(solve_kernel, low, high, ridge, scale),
        out_shape=jax.ShapeDtypeStruct((4, 128), jnp.float32),
        in_specs=[
            pl.BlockSpec(memory_space=pltpu.SMEM),
            pl.BlockSpec(memory_space=pltpu.VMEM),
            pl.BlockSpec(memory_space=pltpu.VMEM),
        ],
        scratch_shapes=[pltpu.VMEM((2, 1024, 128), jnp.float32)],
        name="solve",
        compiler_params=pltpu.CompilerParams(vmem_limit_bytes=40 * 2**20),
    )(spots, mine, theirs)


def sine_coefficients(scale):
    nodes = np.cos((np.arange(64) + 0.5) * np.pi / 64) * 0.25
    powers = np.stack([nodes ** (2 * k) for k in range(4)], axis=1)
    fitted = np.linalg.lstsq(powers, np.sin(2 * np.pi * nodes) / nodes, rcond=None)[0]
    return [float(scale * c) for c in fitted]


def cosine_of_turns(turns, scale):
    turns = turns - jnp.round(turns)
    quarter = 0.25 - jnp.abs(turns)
    square = quarter * quarter
    c = sine_coefficients(scale)
    series = c[2] + square * c[3]
    series = c[1] + square * series
    series = c[0] + square * series
    return quarter * series


def cross(a, b):
    return lax.dot_general(a, b, (((0,), (0,)), ((), ())), preferred_element_type=jnp.float32)


def gram_kernel(blocks, part, scale, spots_ref, x_ref, y_ref, w_ref, phase_ref, send_ref, keep_ref, f_ref, a_ref, b_ref, r_ref):
    step = pl.program_id(0)
    rows = x_ref.shape[0]
    new = lax.rem(step, 2)
    old = 1 - new
    turn = np.float32(1 / (2 * np.pi))
    phase = phase_ref[...] * turn

    def project(s):
        return jnp.dot(x_ref[s * part:(s + 1) * part], w_ref[...], preferred_element_type=jnp.float32)

    def feature(s, projected):
        f_ref[new, s * part:(s + 1) * part] = cosine_of_turns(projected * turn + phase, scale).astype(jnp.bfloat16)

    def gram_left():
        a_ref[...] += cross(f_ref[old, :, :256], f_ref[old, :, :256])

    def gram_rest(k):
        cols = slice(k * 256, (k + 1) * 256)
        b_ref[:, cols] += cross(f_ref[old, :, 256:], f_ref[old, :, cols])
        r_ref[:, cols] += cross(y_ref[...], f_ref[old, :, cols])

    def run(with_features, with_gram):
        jobs = [gram_left, lambda: gram_rest(0), lambda: gram_rest(1)] if with_gram else []
        for s in range(rows // part if with_features else 0):
            projected = project(s)
            if jobs:
                jobs.pop(0)()
            feature(s, projected)
        for job in jobs:
            job()

    @pl.when(step == 0)
    def _():
        a_ref[...] = jnp.zeros_like(a_ref)
        b_ref[...] = jnp.zeros_like(b_ref)
        r_ref[...] = jnp.zeros_like(r_ref)
        run(True, False)

    @pl.when((step > 0) & (step < blocks))
    def _():
        run(True, True)

    @pl.when(step == blocks)
    def _():
        run(False, True)

        def first(ref):
            for k in range(2):
                ref[256 * k:256 * (k + 1)] = a_ref[:, 128 * k:128 * (k + 1)]
            for k in range(4):
                ref[512 + 128 * k:640 + 128 * k] = r_ref[:, 128 * k:128 * (k + 1)]

        def second(ref):
            for k in range(4):
                ref[256 * k:256 * (k + 1)] = b_ref[:, 128 * k:128 * (k + 1)]

        @pl.when(spots_ref[0] == 0)
        def _():
            first(keep_ref)
            second(send_ref)

        @pl.when(spots_ref[0] != 0)
        def _():
            second(keep_ref)
            first(send_ref)


def in_hbm(array):
    return pltpu.with_memory_space_constraint(array, pltpu.HBM)


def local_gram(spots, inputs, frequencies, phases, targets, rows=1024, part=256):
    blocks = inputs.shape[0] // rows
    count = frequencies.shape[1]
    return pl.pallas_call(
        functools.partial(gram_kernel, blocks, part, np.sqrt(2.0 / count)),
        grid=(blocks + 1,),
        in_specs=[
            pl.BlockSpec(memory_space=pltpu.SMEM),
            pl.BlockSpec((rows, 512), lambda i: (jnp.minimum(i, blocks - 1), 0)),
            pl.BlockSpec((rows, 128), lambda i: (jnp.maximum(i - 1, 0), 0)),
            pl.BlockSpec((512, 512), lambda i: (0, 0)),
            pl.BlockSpec((1, 512), lambda i: (0, 0)),
        ],
        out_specs=[pl.BlockSpec((1024, 128), lambda i: (0, 0))] * 2,
        out_shape=[jax.ShapeDtypeStruct((1024, 128), jnp.float32)] * 2,
        scratch_shapes=[
            pltpu.VMEM((2, rows, 512), jnp.bfloat16),
            pltpu.VMEM((256, 256), jnp.float32),
            pltpu.VMEM((256, 512), jnp.float32),
            pltpu.VMEM((128, 512), jnp.float32),
        ],
        name="gram",
        compiler_params=pltpu.CompilerParams(vmem_limit_bytes=50 * 2**20),
    )(spots, inputs, *[in_hbm(v) for v in (targets, frequencies, phases.reshape(1, 512))])


def sum_over_devices(send, keep):
    swap = [(0, 1), (1, 0)]
    half = keep + lax.ppermute(send, "core", swap)
    chunks = lax.all_to_all(half.reshape(64, 16, 128), CHIPS, 0, 0, tiled=True)
    total = jnp.sum(chunks, axis=0, keepdims=True)
    gathered = lax.all_to_all(jnp.broadcast_to(total, (64, 16, 128)), CHIPS, 0, 0, tiled=True)
    mine = gathered.reshape(1024, 128)
    return mine, lax.ppermute(mine, "core", swap)


def body(inputs, frequencies, phases, targets):
    feature_count = frequencies.shape[1]
    total_rows = inputs.shape[0] * 128
    ridge = 0.25 * total_rows / feature_count
    group = lax.axis_index(("z", "x", "core"))
    spots = jnp.stack([lax.axis_index("core"), group // 2 * 8, group % 2, lax.axis_index("y")])
    spots = spots.astype(jnp.int32)
    send, keep = local_gram(spots, inputs, frequencies, phases, targets)
    mine, theirs = sum_over_devices(send, keep)
    return solve(spots, mine, theirs, ridge, np.sqrt(total_rows / feature_count)).T


def solution(mesh):
    split = Mesh(mesh.devices.reshape(4, 4, 2, 4), ("z", "x", "core", "y"))
    rows = ("z", "x", "core", "y")
    return jax.shard_map(
        body,
        mesh=split,
        in_specs=(P(rows, None), P(), P(), P(rows, None)),
        out_specs=P("y", ("z", "x", "core")),
        check_vma=False,
    )
```

```python
import functools

import jax
import jax.numpy as jnp
import numpy as np
from jax import lax
from jax.experimental import pallas as pl
from jax.experimental.pallas import tpu as pltpu
from jax.sharding import Mesh, PartitionSpec as P

CHIPS = ("z", "x", "y")
HIGHEST = lax.Precision.HIGHEST


def dot32(a, b, dims=((1,), (0,))):
    return lax.dot_general(a, b, (dims, ((), ())), precision=HIGHEST, preferred_element_type=jnp.float32)

def halves(v):
    high = v.astype(jnp.bfloat16)
    return high, (v - high.astype(jnp.float32)).astype(jnp.bfloat16)

def dot16(a, b):
    return jnp.dot(a, b, preferred_element_type=jnp.float32)

def dot_split(a, b):
    (ah, al), (bh, bl) = a, b
    return dot16(ah, bh) + (dot16(ah, bl) + dot16(al, bh))

def spectrum_steps(low, high, small):
    middle = 2.0 / (low + high)
    reach = (high - low) / (high + low)
    scales = []
    while reach > small:
        scales.append(2.0 / (2.0 - reach * reach))
        reach = reach * reach / (2.0 - reach * reach)
    return middle, scales

def inverse_of(a, eye, low, high, polish):
    middle, scales = spectrum_steps(low, high, 1e-3)
    y = middle * a
    yy = halves(y)
    x = (2.0 * middle * scales[0]) * eye - (middle * scales[0]) * y
    y = scales[0] * (2.0 * y - dot_split(yy, yy))
    for s in scales[1:-1]:
        yy = halves(y)
        x = s * (2.0 * x - dot_split(halves(x), yy))
        y = s * (2.0 * y - dot_split(yy, yy))
    x = scales[-1] * (2.0 * x - dot_split(halves(x), halves(y)))
    for _ in range(polish):
        miss = eye - dot32(a, x)
        x = x + dot_split(halves(x), halves(miss))
    return x


def unit(n):
    rows = lax.broadcasted_iota(jnp.int32, (n, n), 0)
    cols = lax.broadcasted_iota(jnp.int32, (n, n), 1)
    return jnp.where(rows == cols, 1.0, 0.0).astype(jnp.float32)


def slabs(ref, start, rows=256):
    return jnp.concatenate([ref[start:start + rows], ref[start + rows:start + 2 * rows]], axis=1)


def own_kernel(low, high, ridge, mine_ref, x_ref, b_ref):
    eye = unit(256)
    x_ref[...] = inverse_of(slabs(mine_ref, 0) + ridge * eye, eye, low, high, 2)
    b_ref[...] = slabs(mine_ref, 512).T


def rest_kernel(low, high, ridge, scale, spots_ref, mine_ref, theirs_ref, x_ref, turned_ref, out_ref, b_ref, r_ref):
    pick = pl.multiple_of(spots_ref[1], 8)

    @pl.when(spots_ref[0] == 0)
    def _():
        b_ref[...] = slabs(theirs_ref, 512)
        for k in range(4):
            r_ref[:, 128 * k:128 * (k + 1)] = mine_ref[pl.ds(512 + 128 * k + pick, 8)]

    @pl.when(spots_ref[0] != 0)
    def _():
        b_ref[...] = turned_ref[...]
        for k in range(4):
            slab = (k + 2) % 4
            r_ref[:, 128 * k:128 * (k + 1)] = theirs_ref[pl.ds(512 + 128 * slab + pick, 8)]

    eye = unit(256)
    b = b_ref[...]
    x = x_ref[...]
    t = dot32(b, x)
    s = slabs(theirs_ref, 0) + ridge * eye - dot32(t, b, ((1,), (1,)))
    right = r_ref[:, 256:] - dot32(r_ref[:, :256], t, ((1,), (1,)))
    inverse = halves(inverse_of(s, eye, low, high, 0))
    other = dot_split(halves(right), inverse)
    for _ in range(2):
        other = other + dot_split(halves(right - dot32(other, s)), inverse)
    own = dot32(r_ref[:, :256] - dot32(other, b), x)
    flip = spots_ref[0] != 0
    w = scale * jnp.concatenate([jnp.where(flip, other, own), jnp.where(flip, own, other)], axis=1)
    w = jnp.where(spots_ref[2] == 0, w[:4], w[4:])
    out = w[:, :128]
    for k in range(1, 4):
        out = jnp.where(spots_ref[3] == k, w[:, 128 * k:128 * (k + 1)], out)
    out_ref[...] = out


def solve(spots, mine, theirs, ridge, scale):
    low = 0.98 * ridge
    high = 1.01 * (256 * 8 + 1) * ridge
    vmem = pl.BlockSpec(memory_space=pltpu.VMEM)
    square = jax.ShapeDtypeStruct((256, 256), jnp.float32)
    params = pltpu.CompilerParams(vmem_limit_bytes=40 * 2**20)
    x, turned = pl.pallas_call(
        functools.partial(own_kernel, low, high, ridge),
        out_shape=[square, square],
        in_specs=[vmem],
        out_specs=[vmem, vmem],
        name="own",
        cost_estimate=pl.CostEstimate(flops=5 * 10**9, bytes_accessed=10**6, transcendentals=0),
        compiler_params=params,
    )(mine)
    return pl.pallas_call(
        functools.partial(rest_kernel, low, high, ridge, scale),
        out_shape=jax.ShapeDtypeStruct((4, 128), jnp.float32),
        in_specs=[pl.BlockSpec(memory_space=pltpu.SMEM)] + [vmem] * 4,
        scratch_shapes=[pltpu.VMEM((256, 256), jnp.float32), pltpu.VMEM((8, 512), jnp.float32)],
        name="rest",
        compiler_params=params,
    )(spots, mine, theirs, x, turned)


def sine_coefficients(scale):
    nodes = np.cos((np.arange(64) + 0.5) * np.pi / 64) * 0.25
    powers = np.stack([nodes ** (2 * k) for k in range(4)], axis=1)
    fitted = np.linalg.lstsq(powers, np.sin(2 * np.pi * nodes) / nodes, rcond=None)[0]
    return [float(scale * c) for c in fitted]


def cosine_of_turns(turns, scale):
    turns = turns - jnp.round(turns)
    quarter = 0.25 - jnp.abs(turns)
    square = quarter * quarter
    c = sine_coefficients(scale)
    series = c[2] + square * c[3]
    series = c[1] + square * series
    series = c[0] + square * series
    return quarter * series


def cross(a, b):
    return lax.dot_general(a, b, (((0,), (0,)), ((), ())), preferred_element_type=jnp.float32)


def gram_kernel(blocks, part, scale, spots_ref, x_ref, y_ref, w_ref, phase_ref, send_ref, keep_ref, f_ref, a_ref, b_ref, r_ref):
    step = pl.program_id(0)
    rows = x_ref.shape[0]
    new = lax.rem(step, 2)
    old = 1 - new
    turn = np.float32(1 / (2 * np.pi))
    phase = phase_ref[...] * turn

    def project(s):
        return jnp.dot(x_ref[s * part:(s + 1) * part], w_ref[...], preferred_element_type=jnp.float32)

    def feature(s, projected):
        f_ref[new, s * part:(s + 1) * part] = cosine_of_turns(projected * turn + phase, scale).astype(jnp.bfloat16)

    def gram_late():
        late = jnp.concatenate([f_ref[old, :, 256:], y_ref[...]], axis=1)
        sums = cross(late, f_ref[old])
        b_ref[...] += sums[:256]
        r_ref[...] += sums[256:]

    def gram_left():
        a_ref[...] += cross(f_ref[old, :, :256], f_ref[old, :, :256])

    def run(with_features, with_gram):
        jobs = [gram_late, gram_left] if with_gram else []
        for s in range(rows // part if with_features else 0):
            projected = project(s)
            if jobs:
                jobs.pop(0)()
            feature(s, projected)
        for job in jobs:
            job()

    @pl.when(step == 0)
    def _():
        a_ref[...] = jnp.zeros_like(a_ref)
        b_ref[...] = jnp.zeros_like(b_ref)
        r_ref[...] = jnp.zeros_like(r_ref)
        run(True, False)

    @pl.when((step > 0) & (step < blocks))
    def _():
        run(True, True)

    @pl.when(step == blocks)
    def _():
        run(False, True)

        def first(ref):
            for k in range(2):
                ref[256 * k:256 * (k + 1)] = a_ref[:, 128 * k:128 * (k + 1)]
            for k in range(4):
                ref[512 + 128 * k:640 + 128 * k] = r_ref[:, 128 * k:128 * (k + 1)]

        def second(ref):
            for k in range(4):
                slab = (k + 2) % 4
                ref[256 * k:256 * (k + 1)] = b_ref[:, 128 * slab:128 * (slab + 1)]

        @pl.when(spots_ref[0] == 0)
        def _():
            first(keep_ref)
            second(send_ref)

        @pl.when(spots_ref[0] != 0)
        def _():
            second(keep_ref)
            first(send_ref)


def in_hbm(array):
    return pltpu.with_memory_space_constraint(array, pltpu.HBM)


def local_gram(spots, inputs, frequencies, phases, targets, rows=1024, part=256):
    blocks = inputs.shape[0] // rows
    count = frequencies.shape[1]
    return pl.pallas_call(
        functools.partial(gram_kernel, blocks, part, np.sqrt(2.0 / count)),
        grid=(blocks + 1,),
        in_specs=[
            pl.BlockSpec(memory_space=pltpu.SMEM),
            pl.BlockSpec((rows, 512), lambda i: (jnp.minimum(i, blocks - 1), 0)),
            pl.BlockSpec((rows, 128), lambda i: (jnp.maximum(i - 1, 0), 0)),
            pl.BlockSpec((512, 512), lambda i: (0, 0)),
            pl.BlockSpec((1, 512), lambda i: (0, 0)),
        ],
        out_specs=[pl.BlockSpec((1024, 128), lambda i: (0, 0))] * 2,
        out_shape=[jax.ShapeDtypeStruct((1024, 128), jnp.float32)] * 2,
        scratch_shapes=[
            pltpu.VMEM((2, rows, 512), jnp.bfloat16),
            pltpu.VMEM((256, 256), jnp.float32),
            pltpu.VMEM((256, 512), jnp.float32),
            pltpu.VMEM((128, 512), jnp.float32),
        ],
        name="gram",
        compiler_params=pltpu.CompilerParams(vmem_limit_bytes=50 * 2**20),
    )(spots, inputs, *[in_hbm(v) for v in (targets, frequencies, phases.reshape(1, 512))])


def sum_over_devices(send, keep):
    swap = [(0, 1), (1, 0)]
    half = keep + lax.ppermute(send, "core", swap)
    chunks = lax.all_to_all(half.reshape(64, 16, 128), CHIPS, 0, 0, tiled=True)
    total = jnp.sum(chunks, axis=0, keepdims=True)
    gathered = lax.all_to_all(jnp.broadcast_to(total, (64, 16, 128)), CHIPS, 0, 0, tiled=True)
    mine = gathered.reshape(1024, 128)
    return mine, lax.ppermute(mine, "core", swap)


def body(inputs, frequencies, phases, targets):
    feature_count = frequencies.shape[1]
    total_rows = inputs.shape[0] * 128
    ridge = 0.25 * total_rows / feature_count
    group = lax.axis_index(("z", "x", "core"))
    spots = jnp.stack([lax.axis_index("core"), group // 2 * 8, group % 2, lax.axis_index("y")])
    spots = spots.astype(jnp.int32)
    send, keep = local_gram(spots, inputs, frequencies, phases, targets)
    mine, theirs = sum_over_devices(send, keep)
    return solve(spots, mine, theirs, ridge, np.sqrt(total_rows / feature_count)).T


def solution(mesh):
    split = Mesh(mesh.devices.reshape(4, 4, 2, 4), ("z", "x", "core", "y"))
    rows = ("z", "x", "core", "y")
    return jax.shard_map(
        body,
        mesh=split,
        in_specs=(P(rows, None), P(), P(), P(rows, None)),
        out_specs=P("y", ("z", "x", "core")),
        check_vma=False,
    )
```

```python
import functools

import jax
import jax.numpy as jnp
import numpy as np
from jax import lax
from jax.experimental import pallas as pl
from jax.experimental.pallas import tpu as pltpu
from jax.sharding import Mesh, PartitionSpec as P

CHIPS = ("z", "x", "y")
HIGHEST = lax.Precision.HIGHEST


def dot32(a, b, dims=((1,), (0,))):
    return lax.dot_general(a, b, (dims, ((), ())), precision=HIGHEST, preferred_element_type=jnp.float32)

def halves(v):
    high = v.astype(jnp.bfloat16)
    return high, (v - high.astype(jnp.float32)).astype(jnp.bfloat16)

def dot16(a, b):
    return jnp.dot(a, b, preferred_element_type=jnp.float32)

def dot_split(a, b):
    (ah, al), (bh, bl) = a, b
    return dot16(ah, bh) + (dot16(ah, bl) + dot16(al, bh))

def spectrum_steps(low, high, small):
    middle = 2.0 / (low + high)
    reach = (high - low) / (high + low)
    scales = []
    while reach > small:
        scales.append(2.0 / (2.0 - reach * reach))
        reach = reach * reach / (2.0 - reach * reach)
    return middle, scales

def inverse_of(a, eye, low, high, polish):
    middle, scales = spectrum_steps(low, high, 1e-3)
    y = middle * a
    yy = halves(y)
    x = (2.0 * middle * scales[0]) * eye - (middle * scales[0]) * y
    y = scales[0] * (2.0 * y - dot_split(yy, yy))
    for s in scales[1:-1]:
        yy = halves(y)
        x = s * (2.0 * x - dot_split(halves(x), yy))
        y = s * (2.0 * y - dot_split(yy, yy))
    x = scales[-1] * (2.0 * x - dot_split(halves(x), halves(y)))
    for _ in range(polish):
        miss = eye - dot32(a, x)
        x = x + dot_split(halves(x), halves(miss))
    return x


def unit(n):
    rows = lax.broadcasted_iota(jnp.int32, (n, n), 0)
    cols = lax.broadcasted_iota(jnp.int32, (n, n), 1)
    return jnp.where(rows == cols, 1.0, 0.0).astype(jnp.float32)


def slabs(ref, start, rows=256):
    return jnp.concatenate([ref[start:start + rows], ref[start + rows:start + 2 * rows]], axis=1)


def own_kernel(low, high, ridge, mine_ref, x_ref, b_ref):
    eye = unit(256)
    x_ref[...] = inverse_of(slabs(mine_ref, 0) + ridge * eye, eye, low, high, 2)
    b_ref[...] = slabs(mine_ref, 512).T


def rest_kernel(low, high, ridge, scale, spots_ref, mine_ref, theirs_ref, x_ref, turned_ref, out_ref, b_ref, r_ref):
    pick = pl.multiple_of(spots_ref[1], 8)

    @pl.when(spots_ref[0] == 0)
    def _():
        b_ref[...] = slabs(theirs_ref, 512)
        for k in range(4):
            r_ref[:, 128 * k:128 * (k + 1)] = mine_ref[pl.ds(512 + 128 * k + pick, 8)]

    @pl.when(spots_ref[0] != 0)
    def _():
        b_ref[...] = turned_ref[...]
        for k in range(4):
            slab = (k + 2) % 4
            r_ref[:, 128 * k:128 * (k + 1)] = theirs_ref[pl.ds(512 + 128 * slab + pick, 8)]

    eye = unit(256)
    b = b_ref[...]
    x = x_ref[...]
    t = dot32(b, x)
    s = slabs(theirs_ref, 0) + ridge * eye - dot32(t, b, ((1,), (1,)))
    right = r_ref[:, 256:] - dot32(r_ref[:, :256], t, ((1,), (1,)))
    inverse = halves(inverse_of(s, eye, low, high, 0))
    other = dot_split(halves(right), inverse)
    for _ in range(2):
        other = other + dot_split(halves(right - dot32(other, s)), inverse)
    own = dot32(r_ref[:, :256] - dot32(other, b), x)
    flip = spots_ref[0] != 0
    w = scale * jnp.concatenate([jnp.where(flip, other, own), jnp.where(flip, own, other)], axis=1)
    w = jnp.where(spots_ref[2] == 0, w[:4], w[4:])
    out = w[:, :128]
    for k in range(1, 4):
        out = jnp.where(spots_ref[3] == k, w[:, 128 * k:128 * (k + 1)], out)
    out_ref[...] = out


def solve(spots, mine, theirs, ridge, scale):
    low = 0.98 * ridge
    high = 1.01 * (256 * 8 + 1) * ridge
    vmem = pl.BlockSpec(memory_space=pltpu.VMEM)
    square = jax.ShapeDtypeStruct((256, 256), jnp.float32)
    params = pltpu.CompilerParams(vmem_limit_bytes=40 * 2**20)
    x, turned = pl.pallas_call(
        functools.partial(own_kernel, low, high, ridge),
        out_shape=[square, square],
        in_specs=[vmem],
        out_specs=[vmem, vmem],
        name="own",
        cost_estimate=pl.CostEstimate(flops=5 * 10**9, bytes_accessed=10**6, transcendentals=0),
        compiler_params=params,
    )(mine)
    return pl.pallas_call(
        functools.partial(rest_kernel, low, high, ridge, scale),
        out_shape=jax.ShapeDtypeStruct((4, 128), jnp.float32),
        in_specs=[pl.BlockSpec(memory_space=pltpu.SMEM)] + [vmem] * 4,
        scratch_shapes=[pltpu.VMEM((256, 256), jnp.float32), pltpu.VMEM((8, 512), jnp.float32)],
        name="rest",
        compiler_params=params,
    )(spots, mine, theirs, x, turned)


def sine_coefficients(scale):
    nodes = np.cos((np.arange(64) + 0.5) * np.pi / 64) * 0.25
    powers = np.stack([nodes ** (2 * k) for k in range(4)], axis=1)
    fitted = np.linalg.lstsq(powers, np.sin(2 * np.pi * nodes) / nodes, rcond=None)[0]
    return [float(scale * c) for c in fitted]


def cosine_of_turns(turns, scale):
    turns = turns - jnp.round(turns)
    quarter = 0.25 - jnp.abs(turns)
    square = quarter * quarter
    c = sine_coefficients(scale)
    series = c[2] + square * c[3]
    series = c[1] + square * series
    series = c[0] + square * series
    return quarter * series


def cross(a, b):
    return lax.dot_general(a, b, (((0,), (0,)), ((), ())), preferred_element_type=jnp.float32)


def gram_kernel(steps, part, scale, spots_ref, x_ref, y_old_ref, y_new_ref, w_ref, phase_ref, send_ref, keep_ref, even_ref, odd_ref, a_ref, b_ref, r_ref):
    step = pl.program_id(0)
    rows = even_ref.shape[0]
    turn = np.float32(1 / (2 * np.pi))
    phase = phase_ref[...] * turn

    def half_step(start, new_ref, old_ref, y_ref, with_features, with_gram):
        def project(s):
            some = x_ref[start + s * part:start + (s + 1) * part]
            return jnp.dot(some, w_ref[...], preferred_element_type=jnp.float32)

        def feature(s, projected):
            new_ref[s * part:(s + 1) * part] = cosine_of_turns(projected * turn + phase, scale).astype(jnp.bfloat16)

        def gram_late():
            late = jnp.concatenate([old_ref[:, 256:], y_ref[...]], axis=1)
            sums = cross(late, old_ref[...])
            b_ref[...] += sums[:256]
            r_ref[...] += sums[256:]

        def gram_left():
            a_ref[...] += cross(old_ref[:, :256], old_ref[:, :256])

        jobs = [gram_late, gram_left] if with_gram else []
        for s in range(rows // part if with_features else 0):
            projected = project(s)
            if jobs:
                jobs.pop(0)()
            feature(s, projected)
        for job in jobs:
            job()

    @pl.when(step == 0)
    def _():
        a_ref[...] = jnp.zeros_like(a_ref)
        b_ref[...] = jnp.zeros_like(b_ref)
        r_ref[...] = jnp.zeros_like(r_ref)
        half_step(0, even_ref, odd_ref, y_old_ref, True, False)
        half_step(rows, odd_ref, even_ref, y_new_ref, True, True)

    @pl.when((step > 0) & (step < steps))
    def _():
        half_step(0, even_ref, odd_ref, y_old_ref, True, True)
        half_step(rows, odd_ref, even_ref, y_new_ref, True, True)

    @pl.when(step == steps)
    def _():
        half_step(0, even_ref, odd_ref, y_old_ref, False, True)

        def first(ref):
            for k in range(2):
                ref[256 * k:256 * (k + 1)] = a_ref[:, 128 * k:128 * (k + 1)]
            for k in range(4):
                ref[512 + 128 * k:640 + 128 * k] = r_ref[:, 128 * k:128 * (k + 1)]

        def second(ref):
            for k in range(4):
                slab = (k + 2) % 4
                ref[256 * k:256 * (k + 1)] = b_ref[:, 128 * slab:128 * (slab + 1)]

        @pl.when(spots_ref[0] == 0)
        def _():
            first(keep_ref)
            second(send_ref)

        @pl.when(spots_ref[0] != 0)
        def _():
            second(keep_ref)
            first(send_ref)


def in_hbm(array):
    return pltpu.with_memory_space_constraint(array, pltpu.HBM)


def local_gram(spots, inputs, frequencies, phases, targets, rows=1024, part=512):
    steps = inputs.shape[0] // (2 * rows)
    count = frequencies.shape[1]
    return pl.pallas_call(
        functools.partial(gram_kernel, steps, part, np.sqrt(2.0 / count)),
        grid=(steps + 1,),
        in_specs=[
            pl.BlockSpec(memory_space=pltpu.SMEM),
            pl.BlockSpec((2 * rows, 512), lambda i: (jnp.minimum(i, steps - 1), 0)),
            pl.BlockSpec((rows, 128), lambda i: (jnp.maximum(2 * i - 1, 0), 0)),
            pl.BlockSpec((rows, 128), lambda i: (jnp.minimum(2 * i, 2 * steps - 1), 0)),
            pl.BlockSpec((512, 512), lambda i: (0, 0)),
            pl.BlockSpec((1, 512), lambda i: (0, 0)),
        ],
        out_specs=[pl.BlockSpec((1024, 128), lambda i: (0, 0))] * 2,
        out_shape=[jax.ShapeDtypeStruct((1024, 128), jnp.float32)] * 2,
        scratch_shapes=[
            pltpu.VMEM((rows, 512), jnp.bfloat16),
            pltpu.VMEM((rows, 512), jnp.bfloat16),
            pltpu.VMEM((256, 256), jnp.float32),
            pltpu.VMEM((256, 512), jnp.float32),
            pltpu.VMEM((128, 512), jnp.float32),
        ],
        name="gram",
        compiler_params=pltpu.CompilerParams(vmem_limit_bytes=50 * 2**20),
    )(spots, inputs, *[in_hbm(v) for v in (targets, targets, frequencies, phases.reshape(1, 512))])


def sum_over_devices(send, keep):
    swap = [(0, 1), (1, 0)]
    half = keep + lax.ppermute(send, "core", swap)
    chunks = lax.all_to_all(half.reshape(64, 16, 128), CHIPS, 0, 0, tiled=True)
    total = jnp.sum(chunks, axis=0, keepdims=True)
    gathered = lax.all_to_all(jnp.broadcast_to(total, (64, 16, 128)), CHIPS, 0, 0, tiled=True)
    mine = gathered.reshape(1024, 128)
    return mine, lax.ppermute(mine, "core", swap)


def body(inputs, frequencies, phases, targets):
    feature_count = frequencies.shape[1]
    total_rows = inputs.shape[0] * 128
    ridge = 0.25 * total_rows / feature_count
    group = lax.axis_index(("z", "x", "core"))
    spots = jnp.stack([lax.axis_index("core"), group // 2 * 8, group % 2, lax.axis_index("y")])
    spots = spots.astype(jnp.int32)
    send, keep = local_gram(spots, inputs, frequencies, phases, targets)
    mine, theirs = sum_over_devices(send, keep)
    return solve(spots, mine, theirs, ridge, np.sqrt(total_rows / feature_count)).T


def solution(mesh):
    split = Mesh(mesh.devices.reshape(4, 4, 2, 4), ("z", "x", "core", "y"))
    rows = ("z", "x", "core", "y")
    return jax.shard_map(
        body,
        mesh=split,
        in_specs=(P(rows, None), P(), P(), P(rows, None)),
        out_specs=P("y", ("z", "x", "core")),
        check_vma=False,
    )
```

```python
import functools

import jax
import jax.numpy as jnp
import numpy as np
from jax import lax
from jax.experimental import pallas as pl
from jax.experimental.pallas import tpu as pltpu
from jax.sharding import Mesh, PartitionSpec as P

CHIPS = ("z", "x", "y")
HIGHEST = lax.Precision.HIGHEST


def dot32(a, b, dims=((1,), (0,))):
    return lax.dot_general(a, b, (dims, ((), ())), precision=HIGHEST, preferred_element_type=jnp.float32)

def halves(v):
    high = v.astype(jnp.bfloat16)
    return high, (v - high.astype(jnp.float32)).astype(jnp.bfloat16)

def dot16(a, b):
    return jnp.dot(a, b, preferred_element_type=jnp.float32)

def dot_split(a, b):
    (ah, al), (bh, bl) = a, b
    return dot16(ah, bh) + (dot16(ah, bl) + dot16(al, bh))

def dot_rough(a, b):
    return dot16(a[0], b) + dot16(a[1], b)


def spectrum_steps(low, high, small):
    middle = 2.0 / (low + high)
    reach = (high - low) / (high + low)
    scales = []
    while reach > small:
        scales.append(2.0 / (2.0 - reach * reach))
        reach = reach * reach / (2.0 - reach * reach)
    return middle, scales

def inverse_of(a, eye, low, high, polish):
    middle, scales = spectrum_steps(low, high, 1e-2)
    y = middle * a
    yy = halves(y)
    x = (2.0 * middle * scales[0]) * eye - (middle * scales[0]) * y
    y = scales[0] * (2.0 * y - dot_split(yy, yy))
    for s in scales[1:-3]:
        yy = halves(y)
        x = s * (2.0 * x - dot_split(halves(x), yy))
        y = s * (2.0 * y - dot_split(yy, yy))
    for s in scales[-3:-1]:
        yh = y.astype(jnp.bfloat16)
        x = s * (2.0 * x - dot_rough(halves(x), yh))
        y = s * (2.0 * y - dot16(yh, yh))
    x = scales[-1] * (2.0 * x - dot_rough(halves(x), y.astype(jnp.bfloat16)))
    for _ in range(polish):
        miss = eye - dot32(a, x)
        x = x + dot_rough(halves(x), miss.astype(jnp.bfloat16))
    return x


def unit(n):
    rows = lax.broadcasted_iota(jnp.int32, (n, n), 0)
    cols = lax.broadcasted_iota(jnp.int32, (n, n), 1)
    return jnp.where(rows == cols, 1.0, 0.0).astype(jnp.float32)


def slabs(ref, start, rows=256):
    return jnp.concatenate([ref[start:start + rows], ref[start + rows:start + 2 * rows]], axis=1)


def own_kernel(low, high, ridge, mine_ref, x_ref, b_ref):
    eye = unit(256)
    x_ref[...] = inverse_of(slabs(mine_ref, 0) + ridge * eye, eye, low, high, 1)
    b_ref[...] = slabs(mine_ref, 512).T


def rest_kernel(low, high, ridge, scale, spots_ref, mine_ref, theirs_ref, x_ref, turned_ref, out_ref, b_ref, r_ref):
    pick = pl.multiple_of(spots_ref[1], 8)

    @pl.when(spots_ref[0] == 0)
    def _():
        b_ref[...] = slabs(theirs_ref, 512)
        for k in range(4):
            r_ref[:, 128 * k:128 * (k + 1)] = mine_ref[pl.ds(512 + 128 * k + pick, 8)]

    @pl.when(spots_ref[0] != 0)
    def _():
        b_ref[...] = turned_ref[...]
        for k in range(4):
            slab = (k + 2) % 4
            r_ref[:, 128 * k:128 * (k + 1)] = theirs_ref[pl.ds(512 + 128 * slab + pick, 8)]

    eye = unit(256)
    b = b_ref[...]
    x = x_ref[...]
    a = slabs(mine_ref, 0) + ridge * eye
    xx = halves(x)
    t = dot_split(halves(b), xx)
    t = t + dot_split(halves(b - dot32(t, a)), xx)
    s = slabs(theirs_ref, 0) + ridge * eye - dot32(t, b, ((1,), (1,)))
    right = r_ref[:, 256:] - dot32(r_ref[:, :256], t, ((1,), (1,)))
    inverse = halves(inverse_of(s, eye, low, high, 0))
    other = dot_split(halves(right), inverse)
    for _ in range(2):
        other = other + dot_split(halves(right - dot32(other, s)), inverse)
    right = r_ref[:, :256] - dot32(other, b)
    own = dot_split(halves(right), xx)
    own = own + dot_split(halves(right - dot32(own, a)), xx)
    flip = spots_ref[0] != 0
    w = scale * jnp.concatenate([jnp.where(flip, other, own), jnp.where(flip, own, other)], axis=1)
    w = jnp.where(spots_ref[2] == 0, w[:4], w[4:])
    out = w[:, :128]
    for k in range(1, 4):
        out = jnp.where(spots_ref[3] == k, w[:, 128 * k:128 * (k + 1)], out)
    out_ref[...] = out


def solve(spots, mine, theirs, ridge, scale):
    low = 0.98 * ridge
    high = 1.01 * (256 * 8 + 1) * ridge
    vmem = pl.BlockSpec(memory_space=pltpu.VMEM)
    square = jax.ShapeDtypeStruct((256, 256), jnp.float32)
    params = pltpu.CompilerParams(vmem_limit_bytes=40 * 2**20)
    x, turned = pl.pallas_call(
        functools.partial(own_kernel, low, high, ridge),
        out_shape=[square, square],
        in_specs=[vmem],
        out_specs=[vmem, vmem],
        name="own",
        cost_estimate=pl.CostEstimate(flops=5 * 10**9, bytes_accessed=10**6, transcendentals=0),
        compiler_params=params,
    )(mine)
    return pl.pallas_call(
        functools.partial(rest_kernel, low, high, ridge, scale),
        out_shape=jax.ShapeDtypeStruct((4, 128), jnp.float32),
        in_specs=[pl.BlockSpec(memory_space=pltpu.SMEM)] + [vmem] * 4,
        scratch_shapes=[pltpu.VMEM((256, 256), jnp.float32), pltpu.VMEM((8, 512), jnp.float32)],
        name="rest",
        compiler_params=params,
    )(spots, mine, theirs, x, turned)


def sine_coefficients(scale):
    nodes = np.cos((np.arange(64) + 0.5) * np.pi / 64) * 0.25
    powers = np.stack([nodes ** (2 * k) for k in range(4)], axis=1)
    fitted = np.linalg.lstsq(powers, np.sin(2 * np.pi * nodes) / nodes, rcond=None)[0]
    return [float(scale * c) for c in fitted]


def cosine_of_turns(turns, scale):
    turns = turns - jnp.round(turns)
    quarter = 0.25 - jnp.abs(turns)
    square = quarter * quarter
    c = sine_coefficients(scale)
    series = c[2] + square * c[3]
    series = c[1] + square * series
    series = c[0] + square * series
    return quarter * series


def cross(a, b):
    return lax.dot_general(a, b, (((0,), (0,)), ((), ())), preferred_element_type=jnp.float32)


def gram_kernel(steps, part, scale, spots_ref, x_ref, y_old_ref, y_new_ref, w_ref, phase_ref, send_ref, keep_ref, even_ref, odd_ref, a_ref, b_ref, r_ref):
    step = pl.program_id(0)
    rows = even_ref.shape[0]
    turn = np.float32(1 / (2 * np.pi))
    phase = phase_ref[...] * turn

    def half_step(start, new_ref, old_ref, y_ref, with_features, with_gram):
        def project(s):
            some = x_ref[start + s * part:start + (s + 1) * part]
            return jnp.dot(some, w_ref[...], preferred_element_type=jnp.float32)

        def feature(s, projected):
            new_ref[s * part:(s + 1) * part] = cosine_of_turns(projected * turn + phase, scale).astype(jnp.bfloat16)

        def gram_late():
            late = jnp.concatenate([old_ref[:, 256:], y_ref[...]], axis=1)
            sums = cross(late, old_ref[...])
            b_ref[...] += sums[:256]
            r_ref[...] += sums[256:]

        def gram_left():
            a_ref[...] += cross(old_ref[:, :256], old_ref[:, :256])

        jobs = [gram_late, gram_left] if with_gram else []
        for s in range(rows // part if with_features else 0):
            projected = project(s)
            if jobs:
                jobs.pop(0)()
            feature(s, projected)
        for job in jobs:
            job()

    @pl.when(step == 0)
    def _():
        a_ref[...] = jnp.zeros_like(a_ref)
        b_ref[...] = jnp.zeros_like(b_ref)
        r_ref[...] = jnp.zeros_like(r_ref)
        half_step(0, even_ref, odd_ref, y_old_ref, True, False)
        half_step(rows, odd_ref, even_ref, y_new_ref, True, True)

    @pl.when((step > 0) & (step < steps))
    def _():
        half_step(0, even_ref, odd_ref, y_old_ref, True, True)
        half_step(rows, odd_ref, even_ref, y_new_ref, True, True)

    @pl.when(step == steps)
    def _():
        half_step(0, even_ref, odd_ref, y_old_ref, False, True)

        def first(ref):
            for k in range(2):
                ref[256 * k:256 * (k + 1)] = a_ref[:, 128 * k:128 * (k + 1)]
            for k in range(4):
                ref[512 + 128 * k:640 + 128 * k] = r_ref[:, 128 * k:128 * (k + 1)]

        def second(ref):
            for k in range(4):
                slab = (k + 2) % 4
                ref[256 * k:256 * (k + 1)] = b_ref[:, 128 * slab:128 * (slab + 1)]

        @pl.when(spots_ref[0] == 0)
        def _():
            first(keep_ref)
            second(send_ref)

        @pl.when(spots_ref[0] != 0)
        def _():
            second(keep_ref)
            first(send_ref)


def in_hbm(array):
    return pltpu.with_memory_space_constraint(array, pltpu.HBM)


def local_gram(spots, inputs, frequencies, phases, targets, rows=1024, part=512):
    steps = inputs.shape[0] // (2 * rows)
    count = frequencies.shape[1]
    return pl.pallas_call(
        functools.partial(gram_kernel, steps, part, np.sqrt(2.0 / count)),
        grid=(steps + 1,),
        in_specs=[
            pl.BlockSpec(memory_space=pltpu.SMEM),
            pl.BlockSpec((2 * rows, 512), lambda i: (jnp.minimum(i, steps - 1), 0)),
            pl.BlockSpec((rows, 128), lambda i: (jnp.maximum(2 * i - 1, 0), 0)),
            pl.BlockSpec((rows, 128), lambda i: (jnp.minimum(2 * i, 2 * steps - 1), 0)),
            pl.BlockSpec((512, 512), lambda i: (0, 0)),
            pl.BlockSpec((1, 512), lambda i: (0, 0)),
        ],
        out_specs=[pl.BlockSpec((1024, 128), lambda i: (0, 0))] * 2,
        out_shape=[jax.ShapeDtypeStruct((1024, 128), jnp.float32)] * 2,
        scratch_shapes=[
            pltpu.VMEM((rows, 512), jnp.bfloat16),
            pltpu.VMEM((rows, 512), jnp.bfloat16),
            pltpu.VMEM((256, 256), jnp.float32),
            pltpu.VMEM((256, 512), jnp.float32),
            pltpu.VMEM((128, 512), jnp.float32),
        ],
        name="gram",
        compiler_params=pltpu.CompilerParams(vmem_limit_bytes=50 * 2**20),
    )(spots, inputs, *[in_hbm(v) for v in (targets, targets, frequencies, phases.reshape(1, 512))])


def sum_over_devices(send, keep):
    swap = [(0, 1), (1, 0)]
    half = keep + lax.ppermute(send, "core", swap)
    chunks = lax.all_to_all(half.reshape(64, 16, 128), CHIPS, 0, 0, tiled=True)
    total = jnp.sum(chunks, axis=0, keepdims=True)
    gathered = lax.all_to_all(jnp.broadcast_to(total, (64, 16, 128)), CHIPS, 0, 0, tiled=True)
    mine = gathered.reshape(1024, 128)
    return mine, lax.ppermute(mine, "core", swap)


def body(inputs, frequencies, phases, targets):
    feature_count = frequencies.shape[1]
    total_rows = inputs.shape[0] * 128
    ridge = 0.25 * total_rows / feature_count
    group = lax.axis_index(("z", "x", "core"))
    spots = jnp.stack([lax.axis_index("core"), group // 2 * 8, group % 2, lax.axis_index("y")])
    spots = spots.astype(jnp.int32)
    send, keep = local_gram(spots, inputs, frequencies, phases, targets)
    mine, theirs = sum_over_devices(send, keep)
    return solve(spots, mine, theirs, ridge, np.sqrt(total_rows / feature_count)).T


def solution(mesh):
    split = Mesh(mesh.devices.reshape(4, 4, 2, 4), ("z", "x", "core", "y"))
    rows = ("z", "x", "core", "y")
    return jax.shard_map(
        body,
        mesh=split,
        in_specs=(P(rows, None), P(), P(), P(rows, None)),
        out_specs=P("y", ("z", "x", "core")),
        check_vma=False,
    )
```

```python
import functools

import jax
import jax.numpy as jnp
import numpy as np
from jax import lax
from jax.experimental import pallas as pl
from jax.experimental.pallas import tpu as pltpu
from jax.sharding import Mesh, PartitionSpec as P

CHIPS = ("z", "x", "y")
HIGHEST = lax.Precision.HIGHEST


def dot32(a, b, dims=((1,), (0,))):
    return lax.dot_general(a, b, (dims, ((), ())), precision=HIGHEST, preferred_element_type=jnp.float32)

def halves(v):
    high = v.astype(jnp.bfloat16)
    return high, (v - high.astype(jnp.float32)).astype(jnp.bfloat16)

def dot16(a, b):
    return jnp.dot(a, b, preferred_element_type=jnp.float32)

def dot_split(a, b):
    (ah, al), (bh, bl) = a, b
    return dot16(ah, bh) + (dot16(ah, bl) + dot16(al, bh))

def dot_rough(a, b):
    return dot16(a[0], b) + dot16(a[1], b)


def spectrum_steps(low, high, small):
    middle = 2.0 / (low + high)
    reach = (high - low) / (high + low)
    scales = []
    while reach > small:
        scales.append(2.0 / (2.0 - reach * reach))
        reach = reach * reach / (2.0 - reach * reach)
    return middle, scales

def inverse_of(a, eye, low, high, polish):
    middle, scales = spectrum_steps(low, high, 1e-2)
    y = middle * a
    yy = halves(y)
    x = (2.0 * middle * scales[0]) * eye - (middle * scales[0]) * y
    y = scales[0] * (2.0 * y - dot_split(yy, yy))
    for s in scales[1:-3]:
        yy = halves(y)
        x = s * (2.0 * x - dot_split(halves(x), yy))
        y = s * (2.0 * y - dot_split(yy, yy))
    for s in scales[-3:-1]:
        yh = y.astype(jnp.bfloat16)
        x = s * (2.0 * x - dot_rough(halves(x), yh))
        y = s * (2.0 * y - dot16(yh, yh))
    x = scales[-1] * (2.0 * x - dot_rough(halves(x), y.astype(jnp.bfloat16)))
    for _ in range(polish):
        miss = eye - dot32(a, x)
        x = x + dot_rough(halves(x), miss.astype(jnp.bfloat16))
    return x


def unit(n):
    rows = lax.broadcasted_iota(jnp.int32, (n, n), 0)
    cols = lax.broadcasted_iota(jnp.int32, (n, n), 1)
    return jnp.where(rows == cols, 1.0, 0.0).astype(jnp.float32)


def slabs(ref, start, rows=256):
    return jnp.concatenate([ref[start:start + rows], ref[start + rows:start + 2 * rows]], axis=1)


def own_kernel(low, high, ridge, mine_ref, x_ref, b_ref):
    eye = unit(256)
    x_ref[...] = inverse_of(slabs(mine_ref, 0) + ridge * eye, eye, low, high, 1)
    b_ref[...] = slabs(mine_ref, 512).T


def rest_kernel(low, high, ridge, scale, spots_ref, mine_ref, theirs_ref, x_ref, turned_ref, out_ref, b_ref, r_ref):
    pick = pl.multiple_of(spots_ref[1], 8)

    @pl.when(spots_ref[0] == 0)
    def _():
        b_ref[...] = slabs(theirs_ref, 512)
        for k in range(4):
            r_ref[:, 128 * k:128 * (k + 1)] = mine_ref[pl.ds(512 + 128 * k + pick, 8)]

    @pl.when(spots_ref[0] != 0)
    def _():
        b_ref[...] = turned_ref[...]
        for k in range(4):
            slab = (k + 2) % 4
            r_ref[:, 128 * k:128 * (k + 1)] = theirs_ref[pl.ds(512 + 128 * slab + pick, 8)]

    eye = unit(256)
    b = b_ref[...]
    x = x_ref[...]
    a = slabs(mine_ref, 0) + ridge * eye
    xx = halves(x)
    t = dot_split(halves(b), xx)
    t = t + dot_split(halves(b - dot32(t, a)), xx)
    s = slabs(theirs_ref, 0) + ridge * eye - dot32(t, b, ((1,), (1,)))
    right = r_ref[:, 256:] - dot32(r_ref[:, :256], t, ((1,), (1,)))
    inverse = halves(inverse_of(s, eye, low, high, 0))
    other = dot_split(halves(right), inverse)
    other = other + dot_split(halves(right - dot_split(halves(other), halves(s))), inverse)
    other = other + dot_split(halves(right - dot32(other, s)), inverse)
    right = r_ref[:, :256] - dot32(other, b)
    own = dot_split(halves(right), xx)
    own = own + dot_split(halves(right - dot32(own, a)), xx)
    flip = spots_ref[0] != 0
    w = scale * jnp.concatenate([jnp.where(flip, other, own), jnp.where(flip, own, other)], axis=1)
    w = jnp.where(spots_ref[2] == 0, w[:4], w[4:])
    out = w[:, :128]
    for k in range(1, 4):
        out = jnp.where(spots_ref[3] == k, w[:, 128 * k:128 * (k + 1)], out)
    out_ref[...] = out


def solve(spots, mine, theirs, ridge, scale):
    low = 0.98 * ridge
    high = 1.01 * (256 * 8 + 1) * ridge
    vmem = pl.BlockSpec(memory_space=pltpu.VMEM)
    square = jax.ShapeDtypeStruct((256, 256), jnp.float32)
    params = pltpu.CompilerParams(vmem_limit_bytes=40 * 2**20)
    x, turned = pl.pallas_call(
        functools.partial(own_kernel, low, high, ridge),
        out_shape=[square, square],
        in_specs=[vmem],
        out_specs=[vmem, vmem],
        name="own",
        cost_estimate=pl.CostEstimate(flops=5 * 10**9, bytes_accessed=10**6, transcendentals=0),
        compiler_params=params,
    )(mine)
    return pl.pallas_call(
        functools.partial(rest_kernel, low, high, ridge, scale),
        out_shape=jax.ShapeDtypeStruct((4, 128), jnp.float32),
        in_specs=[pl.BlockSpec(memory_space=pltpu.SMEM)] + [vmem] * 4,
        scratch_shapes=[pltpu.VMEM((256, 256), jnp.float32), pltpu.VMEM((8, 512), jnp.float32)],
        name="rest",
        compiler_params=params,
    )(spots, mine, theirs, x, turned)


def sine_coefficients(scale):
    nodes = np.cos((np.arange(64) + 0.5) * np.pi / 64) * 0.25
    powers = np.stack([nodes ** (2 * k) for k in range(4)], axis=1)
    fitted = np.linalg.lstsq(powers, np.sin(2 * np.pi * nodes) / nodes, rcond=None)[0]
    return [float(scale * c) for c in fitted]


def cosine_of_turns(turns, scale):
    turns = turns - jnp.round(turns)
    quarter = 0.25 - jnp.abs(turns)
    square = quarter * quarter
    c = sine_coefficients(scale)
    series = c[2] + square * c[3]
    series = c[1] + square * series
    series = c[0] + square * series
    return quarter * series


def cross(a, b):
    return lax.dot_general(a, b, (((0,), (0,)), ((), ())), preferred_element_type=jnp.float32)


def gram_kernel(steps, part, scale, spots_ref, x_ref, y_old_ref, y_new_ref, y_last_ref, w_ref, phase_ref, send_ref, keep_ref, even_ref, odd_ref, a_ref, b_ref, r_ref):
    step = pl.program_id(0)
    rows = even_ref.shape[0]
    turn = np.float32(1 / (2 * np.pi))
    phase = phase_ref[...] * turn

    def advance(features, gram):
        jobs = []
        if gram:
            old_ref, y_ref, first_row, count = gram
            some = slice(first_row, first_row + count)

            def gram_late():
                late = jnp.concatenate([old_ref[some, 256:], y_ref[some]], axis=1)
                sums = cross(late, old_ref[some])
                b_ref[...] += sums[:256]
                r_ref[...] += sums[256:]

            def gram_left():
                a_ref[...] += cross(old_ref[some, :256], old_ref[some, :256])

            jobs = [gram_late, gram_left]
        if features:
            start, new_ref, into, count = features
            for s in range(0, count, part):
                projected = jnp.dot(x_ref[start + s:start + s + part], w_ref[...], preferred_element_type=jnp.float32)
                if jobs:
                    jobs.pop(0)()
                made = cosine_of_turns(projected * turn + phase, scale).astype(jnp.bfloat16)
                new_ref[into + s:into + s + part] = made
        for job in jobs:
            job()

    @pl.when(step == 0)
    def _():
        a_ref[...] = jnp.zeros_like(a_ref)
        b_ref[...] = jnp.zeros_like(b_ref)
        r_ref[...] = jnp.zeros_like(r_ref)
        advance((0, even_ref, 0, part), None)
        advance((part, even_ref, part, rows - part), (even_ref, y_new_ref, 0, part))
        advance((rows, odd_ref, 0, rows), (even_ref, y_new_ref, part, rows - part))

    @pl.when((step > 0) & (step < steps - 1))
    def _():
        advance((0, even_ref, 0, rows), (odd_ref, y_old_ref, 0, rows))
        advance((rows, odd_ref, 0, rows), (even_ref, y_new_ref, 0, rows))

    @pl.when(step == steps - 1)
    def _():
        advance((0, even_ref, 0, rows), (odd_ref, y_old_ref, 0, rows))
        advance((rows, odd_ref, 0, rows - part), (even_ref, y_new_ref, 0, rows))
        advance((2 * rows - part, odd_ref, rows - part, part), (odd_ref, y_last_ref, 0, rows - part))
        advance(None, (odd_ref, y_last_ref, rows - part, part))

        def first(ref):
            for k in range(2):
                ref[256 * k:256 * (k + 1)] = a_ref[:, 128 * k:128 * (k + 1)]
            for k in range(4):
                ref[512 + 128 * k:640 + 128 * k] = r_ref[:, 128 * k:128 * (k + 1)]

        def second(ref):
            for k in range(4):
                slab = (k + 2) % 4
                ref[256 * k:256 * (k + 1)] = b_ref[:, 128 * slab:128 * (slab + 1)]

        @pl.when(spots_ref[0] == 0)
        def _():
            first(keep_ref)
            second(send_ref)

        @pl.when(spots_ref[0] != 0)
        def _():
            second(keep_ref)
            first(send_ref)


def in_hbm(array):
    return pltpu.with_memory_space_constraint(array, pltpu.HBM)


def local_gram(spots, inputs, frequencies, phases, targets, rows=1024, part=512):
    steps = inputs.shape[0] // (2 * rows)
    count = frequencies.shape[1]
    return pl.pallas_call(
        functools.partial(gram_kernel, steps, part, np.sqrt(2.0 / count)),
        grid=(steps,),
        in_specs=[
            pl.BlockSpec(memory_space=pltpu.SMEM),
            pl.BlockSpec((2 * rows, 512), lambda i: (i, 0)),
            pl.BlockSpec((rows, 128), lambda i: (jnp.maximum(2 * i - 1, 0), 0)),
            pl.BlockSpec((rows, 128), lambda i: (2 * i, 0)),
            pl.BlockSpec((rows, 128), lambda i: (2 * steps - 1, 0)),
            pl.BlockSpec((512, 512), lambda i: (0, 0)),
            pl.BlockSpec((1, 512), lambda i: (0, 0)),
        ],
        out_specs=[pl.BlockSpec((1024, 128), lambda i: (0, 0))] * 2,
        out_shape=[jax.ShapeDtypeStruct((1024, 128), jnp.float32)] * 2,
        scratch_shapes=[
            pltpu.VMEM((rows, 512), jnp.bfloat16),
            pltpu.VMEM((rows, 512), jnp.bfloat16),
            pltpu.VMEM((256, 256), jnp.float32),
            pltpu.VMEM((256, 512), jnp.float32),
            pltpu.VMEM((128, 512), jnp.float32),
        ],
        name="gram",
        compiler_params=pltpu.CompilerParams(vmem_limit_bytes=50 * 2**20),
    )(spots, inputs, *[in_hbm(v) for v in (targets, targets, targets, frequencies, phases.reshape(1, 512))])


def sum_over_devices(send, keep):
    swap = [(0, 1), (1, 0)]
    half = keep + lax.ppermute(send, "core", swap)
    chunks = lax.all_to_all(half.reshape(64, 16, 128), CHIPS, 0, 0, tiled=True)
    total = jnp.sum(chunks, axis=0, keepdims=True)
    gathered = lax.all_to_all(jnp.broadcast_to(total, (64, 16, 128)), CHIPS, 0, 0, tiled=True)
    mine = gathered.reshape(1024, 128)
    return mine, lax.ppermute(mine, "core", swap)


def body(inputs, frequencies, phases, targets):
    feature_count = frequencies.shape[1]
    total_rows = inputs.shape[0] * 128
    ridge = 0.25 * total_rows / feature_count
    group = lax.axis_index(("z", "x", "core"))
    spots = jnp.stack([lax.axis_index("core"), group // 2 * 8, group % 2, lax.axis_index("y")])
    spots = spots.astype(jnp.int32)
    send, keep = local_gram(spots, inputs, frequencies, phases, targets)
    mine, theirs = sum_over_devices(send, keep)
    return solve(spots, mine, theirs, ridge, np.sqrt(total_rows / feature_count)).T


def solution(mesh):
    split = Mesh(mesh.devices.reshape(4, 4, 2, 4), ("z", "x", "core", "y"))
    rows = ("z", "x", "core", "y")
    return jax.shard_map(
        body,
        mesh=split,
        in_specs=(P(rows, None), P(), P(), P(rows, None)),
        out_specs=P("y", ("z", "x", "core")),
        check_vma=False,
    )
```
